32 devices in a mesh: ctx: 8 (over y, x, core), head: 4 (over z).
Axes of the slice: x: 2, y: 2, z: 4, core: 2. Of those that a mesh axis runs over, the one named last changes fastest.
Arguments:
- join_states: bfloat16 [2048, 4096], P('ctx'), may hold values from -6 to 6
- query_weight: bfloat16 [4096, 4096], P(None, 'head'), may hold values from -0.09375 to 0.09375
- out_weight: bfloat16 [4096, 4096], P('head'), may hold values from -0.5 to 0.5
- outline_keys: bfloat16 [8, 4096, 128], P(None, 'ctx'), may hold values from -180 to 180
- outline_values: bfloat16 [8, 4096, 128], P(None, 'ctx'), may hold values from -6 to 6
- branch_keys: bfloat16 [8, 8192, 128], P(None, 'ctx'), may hold values from -6 to 6
- branch_values: bfloat16 [8, 8192, 128], P(None, 'ctx'), may hold values from -6 to 6
- branch_lengths: int32 [8], replicated, may hold values from 0 to 1024, as said below
- visibility: int32 [64, 8], replicated, may hold values 0 or 1
Outputs:
- attention_out: bfloat16 [2048, 4096], P('ctx', 'head')
The draws below stay inside these ranges and needn't reach their ends.
Inputs may be any that keep to these rules, and one draw needn't show every extreme that they name: `branch_lengths`: exactly one branch in each draw has 1024 live positions.
All inputs are finite; a program needn't handle non-finite values.
Results may differ from the reference program's by a relative error of at most 0.025.
Values may be sent and summed in bfloat16 or wider, within the bound.
A program may use at most 128 MiB of HBM per device.

```python
import jax
import jax.numpy as jnp
from jax import lax

D = 4096
QH = 32
KVH = 8
HD = 128
JSPAN = 32
BR = 1024
BRANCHES = 8
OUTLINE = 4096
JOIN = 2048
JBLK = 64


def draw_outline_keys(key, part):
    base = jnp.clip(jax.random.normal(key, (KVH, OUTLINE, HD), jnp.float32), -6.0, 6.0)
    return base.astype(jnp.bfloat16)


def draw_branch_lengths(key, part):
    drawn = jax.random.randint(key, (BRANCHES,), 0, BR + 1)
    chosen = jax.random.randint(jax.random.fold_in(key, 3), (), 0, BRANCHES)
    return jnp.where(jnp.arange(BRANCHES) == chosen, BR, drawn).astype(jnp.int32)


def touch_ends(values, own_key, low, largest):
    extent = values.shape
    index_at = [jax.random.randint(jax.random.fold_in(own_key, axis), (), 0, extent[axis]) for axis in range(len(extent))]
    values = values.at[tuple(index_at)].set(low)
    longest = extent.index(max(extent))
    index_at[longest] = (index_at[longest] + 1) % extent[longest]
    return values.at[tuple(index_at)].set(largest)


def steps_of(own_key, shape, pieces, low, high):
    factor_of, own = 1.0, jax.random.fold_in(own_key, 6)
    for position, shards_of in pieces:
        heights = jnp.exp(jax.random.uniform(jax.random.fold_in(own, position), (shards_of,), jnp.float32, low / len(pieces), high / len(pieces)))
        factor_of = factor_of * jnp.repeat(heights, shape[position] // shards_of).reshape([-1 if axis == position else 1 for axis in range(len(shape))])
    return factor_of


def bell_draw(key, shape, deviation, most, shards=(), kind=jnp.bfloat16):
    values = jax.random.normal(key, shape, jnp.float32) * deviation
    if len(shards) > 0:
        values = steps_of(key, shape, shards, -0.22, 0.18) * values
    return jnp.clip(values, min=-most, max=most).astype(kind)


def setup_inputs(seed: int = 0) -> dict:
    key_of = jax.random.split(jax.random.key(seed), 10)
    return {
        "join_states": bell_draw(key_of[0], (JOIN, D), 1.0, 6.0, ((0, 8),)),
        "query_weight": bell_draw(key_of[1], (D, QH * HD), D ** -0.5, 0.09375, ((1, 4),)),
        "out_weight": bell_draw(key_of[2], (QH * HD, D), HD ** -0.5, 0.5, ((0, 4),)),
        "outline_keys": draw_outline_keys(jax.random.fold_in(key_of[9], 71), 0),
        "outline_values": bell_draw(key_of[4], (KVH, OUTLINE, HD), 1.0, 6.0, ((1, 8),)),
        "branch_keys": bell_draw(key_of[5], (KVH, BR * BRANCHES, HD), 1.0, 6.0, ((1, 8),)),
        "branch_values": bell_draw(key_of[6], (KVH, BR * BRANCHES, HD), 1.0, 6.0, ((1, 8),)),
        "branch_lengths": draw_branch_lengths(jax.random.fold_in(key_of[9], 71), 0),
        "visibility": touch_ends((jax.random.randint(key_of[8], (JBLK, BRANCHES), 0, 2) < 1).astype(jnp.int32), jax.random.fold_in(key_of[8], 1), 0, 1),
    }


ROPE_BASE = 500000.0
NEG_FILL = -1e30


def rope(queries, first):
    rows = queries.shape[0]
    width = queries.shape[-1]
    half = width // 2
    freq = ROPE_BASE ** (-(jnp.arange(half, dtype=jnp.float32) * 2.0) / width)
    place = (first + jnp.arange(rows)).astype(jnp.float32)
    angle = place[:, None, None] * freq[None, None, :]
    cosine = jnp.cos(angle)
    sine = jnp.sin(angle)
    lower = queries[..., :half]
    upper = queries[..., half:]
    return jnp.concatenate([lower * cosine - upper * sine, upper * cosine + lower * sine], axis=-1)


def reference(join_states, query_weight, out_weight, outline_keys, outline_values, branch_keys, branch_values, branch_lengths, visibility):
    queries = jnp.dot(join_states, query_weight, preferred_element_type=jnp.float32).reshape(JOIN, QH, HD)
    rotated = rope(queries, OUTLINE + BR).astype(jnp.bfloat16)
    keys = jnp.concatenate([outline_keys, branch_keys], axis=1)
    values = jnp.concatenate([outline_values, branch_values], axis=1)
    place = jnp.arange(BR * BRANCHES, dtype=jnp.int32)
    owner = place // BR
    inside = (place % BR) < branch_lengths[owner]
    seen = jnp.repeat(visibility, JSPAN, axis=0)[:, owner]
    branch_visible = (seen == 1) & inside[None, :]
    visible = jnp.concatenate([jnp.ones((JOIN, OUTLINE), dtype=bool), branch_visible], axis=1)
    scale = HD ** -0.5

    def one_head(head):
        query = lax.dynamic_index_in_dim(rotated, head, 1, keepdims=False)
        group = head // (QH // KVH)
        key = lax.dynamic_index_in_dim(keys, group, 0, keepdims=False)
        value = lax.dynamic_index_in_dim(values, group, 0, keepdims=False)
        scores = jnp.dot(query, key.T, preferred_element_type=jnp.float32) * scale
        scores = jnp.where(visible, scores, NEG_FILL)
        best = jnp.max(scores, axis=-1, keepdims=True)
        weights = jnp.where(visible, jnp.exp(scores - best), 0.0)
        total = jnp.sum(weights, axis=-1, keepdims=True)
        mixed = jnp.dot(weights.astype(jnp.bfloat16), value, preferred_element_type=jnp.float32) / total
        return mixed.astype(jnp.bfloat16)

    heads = lax.map(one_head, jnp.arange(QH, dtype=jnp.int32))
    mixed = jnp.transpose(heads, (1, 0, 2)).reshape(JOIN, QH * HD)
    return jnp.dot(mixed, out_weight, preferred_element_type=jnp.float32).astype(jnp.bfloat16)
```

```python
import functools

import jax
import jax.numpy as jnp
from jax import lax
from jax.experimental import pallas as pl
from jax.experimental.pallas import tpu as pltpu
from jax.sharding import PartitionSpec as P

JSPAN = 32
ROPE_BASE = 500000.0
LOG2E = 1.4426950408889634
HIDE = 1e30
CHUNK = 512
CHAINS = 2
MIB = 1 << 20


def rope_tables(rows, width, first, scale):
    half = width // 2
    freq = ROPE_BASE ** (-(jnp.arange(half, dtype=jnp.float32) * 2.0) / width)
    place = (first + jnp.arange(rows)).astype(jnp.float32)
    angle = place[:, None] * freq[None, :]
    cosine = jnp.cos(angle) * scale
    sine = jnp.sin(angle) * scale
    return jnp.concatenate([cosine, cosine], axis=1), jnp.concatenate([-sine, sine], axis=1)


def attend_kernel(per_kv, blocks_each, at_ref, lengths_ref, seen_ref, q_ref, ok_ref, ov_ref, bk_ref, bv_ref,
                  o_ref, stat_ref, ov_wide, bv_wide, order):
    width = ok_ref.shape[2]
    me = at_ref[1]
    length = lengths_ref[me]
    blocks = q_ref.shape[0] // JSPAN
    branch_most = bk_ref.shape[1]
    chunk = min(CHUNK, branch_most)
    ov_wide[:, :width] = ov_ref[0]
    ov_wide[:, width:] = jnp.ones((ov_ref.shape[1], width), jnp.bfloat16)
    bv_wide[:, :width] = bv_ref[0]
    bv_wide[:, width:] = jnp.ones((branch_most, width), jnp.bfloat16)

    def place(block, ends):
        front, back = ends
        hit = seen_ref[block, me] == 1
        order[jnp.where(hit, front, back)] = block
        step = hit.astype(jnp.int32)
        return front + step, back - 1 + step

    seen_count, _ = lax.fori_loop(0, blocks, place, (jnp.int32(0), jnp.int32(blocks - 1)))

    def scores(query, keys):
        return lax.dot_general(query, keys, (((1,), (1,)), ((), ())), preferred_element_type=jnp.float32)

    tile = blocks_each * JSPAN
    per_turn = CHAINS * blocks_each

    def turn(step, _):
        base = step * per_turn
        starts, queries, states, shown = [], [], [], []
        row = lax.broadcasted_iota(jnp.int32, (per_kv * tile, 1), 0)
        slot = (row // JSPAN) % blocks_each
        for chain in range(CHAINS):
            first = base + chain * blocks_each
            at = [pl.multiple_of(order[first + j] * JSPAN, JSPAN) for j in range(blocks_each)]
            starts.append(at)
            queries.append(jnp.concatenate(
                [q_ref[pl.ds(at[j], JSPAN), h * width:(h + 1) * width] for h in range(per_kv) for j in range(blocks_each)],
                axis=0))
            shown.append(first + slot < seen_count)
        for chain in range(CHAINS):
            s = scores(queries[chain], ok_ref[0])
            best = jnp.max(s, axis=1, keepdims=True)
            weights = jnp.exp2(s - best).astype(jnp.bfloat16)
            states += [best, jnp.dot(weights, ov_wide[...], preferred_element_type=jnp.float32)]

        def more(part, state):
            begin = pl.multiple_of(part * chunk, chunk)
            keys = bk_ref[0, pl.ds(begin, chunk), :]
            values = bv_wide[pl.ds(begin, chunk), :]
            place_in = begin + lax.broadcasted_iota(jnp.int32, (1, chunk), 1)
            bias = jnp.where(place_in < length, 0.0, -HIDE)
            out = []
            for chain in range(CHAINS):
                best, acc = state[2 * chain], state[2 * chain + 1]
                s = scores(queries[chain], keys) + bias
                grown = jnp.maximum(best, jnp.max(s, axis=1, keepdims=True))
                new_best = jnp.where(shown[chain], grown, best)
                weights = jnp.exp2(s - jnp.where(shown[chain], grown, HIDE)).astype(jnp.bfloat16)
                acc = acc * jnp.exp2(best - new_best) + jnp.dot(weights, values, preferred_element_type=jnp.float32)
                out += [new_best, acc]
            return tuple(out)

        parts = jnp.where(base < seen_count, (length + chunk - 1) // chunk, 0)
        states = lax.fori_loop(0, parts, more, tuple(states))
        for chain in range(CHAINS):
            best, acc = states[2 * chain], states[2 * chain + 1]
            total = acc[:, width:]
            part_out = (acc[:, :width] / total).astype(o_ref.dtype)
            logs = best + jnp.log2(total[:, :1])
            for h in range(per_kv):
                for j in range(blocks_each):
                    here = (h * blocks_each + j) * JSPAN
                    rows = pl.ds(starts[chain][j], JSPAN)
                    o_ref[rows, h * width:(h + 1) * width] = part_out[here:here + JSPAN]
                    stat_ref[rows, h:h + 1] = logs[here:here + JSPAN]
        return 0

    lax.fori_loop(0, blocks // per_turn, turn, 0)


def attend(query, kv, me, lengths, seen, outline_keys, outline_values, branch_keys, branch_values):
    rows, columns = query.shape
    width = outline_keys.shape[2]
    per_kv = columns // width
    outline_here, branch_most = outline_keys.shape[1], branch_keys.shape[1]
    whole = lambda i, at, lens, vis: (0, 0)
    one = lambda i, at, lens, vis: (at[0], 0, 0)
    keys_all = outline_here + branch_most // 2
    return pl.pallas_call(
        functools.partial(attend_kernel, per_kv, 2),
        out_shape=(jax.ShapeDtypeStruct((rows, columns), jnp.bfloat16), jax.ShapeDtypeStruct((rows, per_kv), jnp.float32)),
        grid_spec=pltpu.PrefetchScalarGridSpec(
            num_scalar_prefetch=3,
            grid=(1,),
            in_specs=[
                pl.BlockSpec((rows, columns), whole),
                pl.BlockSpec((1, outline_here, width), one),
                pl.BlockSpec((1, outline_here, width), one),
                pl.BlockSpec((1, branch_most, width), one),
                pl.BlockSpec((1, branch_most, width), one),
            ],
            out_specs=(pl.BlockSpec((rows, columns), whole), pl.BlockSpec((rows, per_kv), whole)),
            scratch_shapes=[
                pltpu.VMEM((outline_here, 2 * width), jnp.bfloat16),
                pltpu.VMEM((branch_most, 2 * width), jnp.bfloat16),
                pltpu.SMEM((rows // JSPAN,), jnp.int32),
            ],
        ),
        compiler_params=pltpu.CompilerParams(vmem_limit_bytes=40 * MIB),
        cost_estimate=pl.CostEstimate(
            flops=rows * columns * keys_all * 8, bytes_accessed=4 * rows * columns, transcendentals=rows * per_kv * keys_all),
        name="attend",
    )(jnp.stack([kv, me]).astype(jnp.int32), lengths, seen, query, outline_keys, outline_values, branch_keys, branch_values)


def body(join_states, query_weight, out_weight, outline_keys, outline_values, branch_keys, branch_values, branch_lengths, visibility):
    width = outline_keys.shape[2]
    head_count = query_weight.shape[1] // width
    group = head_count * lax.axis_size("head") // outline_keys.shape[0]
    kv_local = max(1, head_count // group)
    per_kv = head_count // kv_local
    kv_start = lax.axis_index("head") * head_count // group
    rows = join_states.shape[0]
    n_ctx = lax.axis_size("ctx")
    me = lax.axis_index("ctx")
    first = outline_keys.shape[1] * n_ctx + branch_keys.shape[1] + me * rows
    cosine, sine = rope_tables(rows, width, first, width ** (-0.5) * LOG2E)
    columns = per_kv * width
    gathered = []
    for kv in range(kv_local):
        queries = jnp.dot(join_states, query_weight[:, kv * columns:(kv + 1) * columns], preferred_element_type=jnp.float32)
        queries = queries.reshape(rows, per_kv, width)
        turned = jnp.concatenate([queries[..., width // 2:], queries[..., :width // 2]], axis=-1)
        rotated = (queries * cosine[:, None, :] + turned * sine[:, None, :]).astype(jnp.bfloat16)
        gathered.append(lax.all_gather(rotated.reshape(rows, columns), "ctx", axis=0, tiled=True))
    parts, logs = [], []
    for kv in range(kv_local):
        part, log = attend(gathered[kv], kv_start + kv, me, branch_lengths, visibility,
                           outline_keys, outline_values, branch_keys, branch_values)
        parts.append(lax.all_to_all(part, "ctx", 0, 0, tiled=True).reshape(n_ctx, rows, per_kv, width))
        logs.append(log)
    logs = lax.all_to_all(jnp.concatenate(logs, axis=1), "ctx", 0, 0, tiled=True).reshape(n_ctx, rows, kv_local, per_kv)
    share = jnp.exp2(logs - jnp.max(logs, axis=0, keepdims=True))
    share = share / jnp.sum(share, axis=0, keepdims=True)
    mixed = [jnp.sum(share[:, :, kv, :, None] * parts[kv].astype(jnp.float32), axis=0).astype(jnp.bfloat16).reshape(rows, columns)
             for kv in range(kv_local)]
    mixed = jnp.concatenate(mixed, axis=1)
    partial_out = jnp.dot(mixed, out_weight, preferred_element_type=jnp.float32)
    return lax.psum_scatter(partial_out.astype(jnp.bfloat16), "head", scatter_dimension=1, tiled=True)


def solution(mesh):
    return jax.shard_map(
        body,
        mesh=mesh,
        in_specs=(P("ctx", None), P(None, "head"), P("head", None), P(None, "ctx", None), P(None, "ctx", None),
                  P(None, "ctx", None), P(None, "ctx", None), P(), P()),
        out_specs=P("ctx", "head"),
        check_vma=False,
    )
```

```python
import functools

import jax
import jax.numpy as jnp
from jax import lax
from jax.experimental import pallas as pl
from jax.experimental.pallas import tpu as pltpu
from jax.sharding import PartitionSpec as P

JSPAN = 32
ROPE_BASE = 500000.0
LOG2E = 1.4426950408889634
HIDE = 1e30
CHUNK = 512
CHAINS = 2
PAD = 16
MIB = 1 << 20


def rope_tables(rows, width, first, scale):
    half = width // 2
    freq = ROPE_BASE ** (-(jnp.arange(half, dtype=jnp.float32) * 2.0) / width)
    place = (first + jnp.arange(rows)).astype(jnp.float32)
    angle = place[:, None] * freq[None, :]
    cosine = jnp.cos(angle) * scale
    sine = jnp.sin(angle) * scale
    return jnp.concatenate([cosine, cosine], axis=1), jnp.concatenate([-sine, sine], axis=1)


def attend_kernel(per_kv, blocks_each, at_ref, lengths_ref, seen_ref, q_ref, ok_ref, ov_ref, bk_ref, bv_ref,
                  o_ref, stat_ref, ov_turned, bv_turned, order):
    width = ok_ref.shape[2]
    me = at_ref[1]
    length = lengths_ref[me]
    blocks = q_ref.shape[0] // JSPAN
    branch_most = bk_ref.shape[1]
    chunk = min(CHUNK, branch_most)
    ov_turned[:width, :] = ov_ref[0].T
    ov_turned[width:, :] = jnp.ones((PAD, ov_ref.shape[1]), jnp.bfloat16)
    for part in range(branch_most // chunk):
        bv_turned[part, :width, :] = bv_ref[0, part * chunk:(part + 1) * chunk].T
        bv_turned[part, width:, :] = jnp.ones((PAD, chunk), jnp.bfloat16)

    def place(block, ends):
        front, back = ends
        hit = seen_ref[block, me] == 1
        order[jnp.where(hit, front, back)] = block
        step = hit.astype(jnp.int32)
        return front + step, back - 1 + step

    seen_count, _ = lax.fori_loop(0, blocks, place, (jnp.int32(0), jnp.int32(blocks - 1)))

    def scores(keys, query):
        return lax.dot_general(keys, query, (((1,), (1,)), ((), ())), preferred_element_type=jnp.float32)

    tile = blocks_each * JSPAN
    per_turn = CHAINS * blocks_each

    def turn(step, _):
        base = step * per_turn
        starts, queries, states, shown = [], [], [], []
        column = lax.broadcasted_iota(jnp.int32, (1, per_kv * tile), 1)
        slot = (column // JSPAN) % blocks_each
        for chain in range(CHAINS):
            first = base + chain * blocks_each
            at = [pl.multiple_of(order[first + j] * JSPAN, JSPAN) for j in range(blocks_each)]
            starts.append(at)
            queries.append(jnp.concatenate(
                [q_ref[pl.ds(at[j], JSPAN), h * width:(h + 1) * width] for h in range(per_kv) for j in range(blocks_each)],
                axis=0))
            shown.append(first + slot < seen_count)
        for chain in range(CHAINS):
            s = scores(ok_ref[0], queries[chain])
            best = jnp.max(s, axis=0, keepdims=True)
            weights = jnp.exp2(s - best).astype(jnp.bfloat16)
            states += [best, jnp.dot(ov_turned[...], weights, preferred_element_type=jnp.float32)]

        def more(part, state):
            begin = pl.multiple_of(part * chunk, chunk)
            keys = bk_ref[0, pl.ds(begin, chunk), :]
            values = bv_turned[part]
            place_in = begin + lax.broadcasted_iota(jnp.int32, (chunk, 1), 0)
            bias = jnp.where(place_in < length, 0.0, -HIDE)
            out = []
            for chain in range(CHAINS):
                best, acc = state[2 * chain], state[2 * chain + 1]
                s = scores(keys, queries[chain]) + bias
                grown = jnp.maximum(best, jnp.max(s, axis=0, keepdims=True))
                new_best = jnp.where(shown[chain], grown, best)
                weights = jnp.exp2(s - jnp.where(shown[chain], grown, HIDE)).astype(jnp.bfloat16)
                acc = acc * jnp.exp2(best - new_best) + jnp.dot(values, weights, preferred_element_type=jnp.float32)
                out += [new_best, acc]
            return tuple(out)

        parts = jnp.where(base < seen_count, (length + chunk - 1) // chunk, 0)
        states = lax.fori_loop(0, parts, more, tuple(states))
        for chain in range(CHAINS):
            best, acc = states[2 * chain], states[2 * chain + 1]
            total = acc[width:width + 8]
            part_out = (acc[:width] * (1.0 / total[:1])).T.astype(o_ref.dtype)
            logs = jnp.concatenate([best + jnp.log2(total), jnp.zeros((width - 8, per_kv * tile), jnp.float32)], axis=0).T
            for h in range(per_kv):
                for j in range(blocks_each):
                    here = (h * blocks_each + j) * JSPAN
                    rows = pl.ds(starts[chain][j], JSPAN)
                    o_ref[rows, h * width:(h + 1) * width] = part_out[here:here + JSPAN]
                    stat_ref[rows, h:h + 1] = logs[here:here + JSPAN, :1]
        return 0

    lax.fori_loop(0, blocks // per_turn, turn, 0)


def attend(query, kv, me, lengths, seen, outline_keys, outline_values, branch_keys, branch_values):
    rows, columns = query.shape
    width = outline_keys.shape[2]
    per_kv = columns // width
    outline_here, branch_most = outline_keys.shape[1], branch_keys.shape[1]
    whole = lambda i, at, lens, vis: (0, 0)
    one = lambda i, at, lens, vis: (at[0], 0, 0)
    keys_all = outline_here + branch_most // 2
    return pl.pallas_call(
        functools.partial(attend_kernel, per_kv, 2),
        out_shape=(jax.ShapeDtypeStruct((rows, columns), jnp.bfloat16), jax.ShapeDtypeStruct((rows, per_kv), jnp.float32)),
        grid_spec=pltpu.PrefetchScalarGridSpec(
            num_scalar_prefetch=3,
            grid=(1,),
            in_specs=[
                pl.BlockSpec((rows, columns), whole),
                pl.BlockSpec((1, outline_here, width), one),
                pl.BlockSpec((1, outline_here, width), one),
                pl.BlockSpec((1, branch_most, width), one),
                pl.BlockSpec((1, branch_most, width), one),
            ],
            out_specs=(pl.BlockSpec((rows, columns), whole), pl.BlockSpec((rows, per_kv), whole)),
            scratch_shapes=[
                pltpu.VMEM((width + PAD, outline_here), jnp.bfloat16),
                pltpu.VMEM((branch_most // min(CHUNK, branch_most), width + PAD, min(CHUNK, branch_most)), jnp.bfloat16),
                pltpu.SMEM((rows // JSPAN,), jnp.int32),
            ],
        ),
        compiler_params=pltpu.CompilerParams(vmem_limit_bytes=60 * MIB),
        cost_estimate=pl.CostEstimate(
            flops=rows * columns * keys_all * 8, bytes_accessed=4 * rows * columns, transcendentals=rows * per_kv * keys_all),
        name="attend",
    )(jnp.stack([kv, me]).astype(jnp.int32), lengths, seen, query, outline_keys, outline_values, branch_keys, branch_values)


def return_kernel(n_ctx, kv_local, heads, *refs):
    parts = refs[:kv_local]
    logs_ref, mixed_ref, near, near_logs, joined, joined_logs, far, far_logs = refs[kv_local:kv_local + 8]
    near_sems, far_sems = refs[kv_local + 8:]
    rows, columns = near.shape[2:]
    width = kv_local * columns // heads
    per_kv = columns // width
    chips = n_ctx // 2
    me = lax.axis_index("ctx")
    chip, core = me // 2, me % 2
    sibling = chip * 2 + 1 - core

    def peer(j):
        return ((chip + j) % chips) * 2

    def copy(src, dst, sems, which, device):
        return pltpu.make_async_remote_copy(
            src_ref=src, dst_ref=dst, send_sem=sems.at[0, which], recv_sem=sems.at[1, which],
            device_id={"ctx": device}, device_id_type=pl.DeviceIdType.MESH)

    barrier = pltpu.get_barrier_semaphore()
    pl.semaphore_signal(barrier, inc=1, device_id={"ctx": sibling}, device_id_type=pl.DeviceIdType.MESH)
    for j in range(1, chips):
        pl.semaphore_signal(barrier, inc=1, device_id={"ctx": peer(j) + core}, device_id_type=pl.DeviceIdType.MESH)
    pl.semaphore_wait(barrier, chips)

    def spread(shares):
        filled = jnp.concatenate([shares, jnp.zeros((128 - shares.shape[0], rows), jnp.float32)], axis=0)
        return filled.T

    sequence = [(j + 1) % chips for j in range(chips)]
    sequence = sequence[::-1][1:] + [0] if chips > 1 else sequence
    near_copies = {}
    for j in sequence:
        block = peer(j) + 1 - core
        mine = pl.ds(pl.multiple_of(block * rows, rows), rows)
        group = [copy(logs_ref.at[block], near_logs.at[j], near_sems, j * (kv_local + 1) + kv_local, sibling)]
        for kv in range(kv_local):
            group.append(copy(parts[kv].at[mine], near.at[j, kv], near_sems, j * (kv_local + 1) + kv, sibling))
        for c in group:
            c.start()
        near_copies[j] = group
    far_copies = {}
    for j in sequence:
        for c in near_copies[j]:
            c.wait_recv()
        block = peer(j) + core
        own, other = logs_ref[block], near_logs[j]
        top = jnp.maximum(own, other)
        own_share, other_share = jnp.exp2(own - top), jnp.exp2(other - top)
        total = own_share + other_share
        joined_logs[j] = top + jnp.log2(total)
        own_wide, other_wide = spread(own_share / total), spread(other_share / total)
        mine = pl.ds(pl.multiple_of(block * rows, rows), rows)
        for kv in range(kv_local):
            for h in range(per_kv):
                at, head = slice(h * width, (h + 1) * width), kv * per_kv + h
                value = (parts[kv][mine, at].astype(jnp.float32) * own_wide[:, head:head + 1]
                         + near[j, kv, :, at].astype(jnp.float32) * other_wide[:, head:head + 1])
                joined[j, kv, :, at] = value.astype(jnp.bfloat16)
        if j > 0:
            group = [copy(joined_logs.at[j], far_logs.at[j - 1], far_sems, 2 * (j - 1) + 1, peer(j) + core),
                     copy(joined.at[j], far.at[j - 1], far_sems, 2 * (j - 1), peer(j) + core)]
            for c in group:
                c.start()
            far_copies[j] = group
    for j in range(1, chips):
        for c in far_copies[j]:
            c.wait_recv()
    every = [joined_logs[0]] + [far_logs[j] for j in range(chips - 1)]
    top = functools.reduce(jnp.maximum, every)
    shares = [jnp.exp2(x - top) for x in every]
    total = functools.reduce(jnp.add, shares)
    wide = [spread(x / total) for x in shares]
    for kv in range(kv_local):
        for h in range(per_kv):
            at, head = slice(h * width, (h + 1) * width), kv * per_kv + h
            value = joined[0, kv, :, at].astype(jnp.float32) * wide[0][:, head:head + 1]
            for j in range(chips - 1):
                value += far[j, kv, :, at].astype(jnp.float32) * wide[j + 1][:, head:head + 1]
            mixed_ref[:, head * width:(head + 1) * width] = value.astype(jnp.bfloat16)
    for j in sequence:
        for c in near_copies[j] + far_copies.get(j, []):
            c.wait_send()


def give_back(parts, logs, n_ctx, heads):
    kv_local = len(parts)
    rows, columns = parts[0].shape[0] // n_ctx, parts[0].shape[1]
    chips = n_ctx // 2
    fars = max(chips - 1, 1)
    tall = logs.shape[1]
    vmem = pl.BlockSpec(memory_space=pltpu.VMEM)
    return pl.pallas_call(
        functools.partial(return_kernel, n_ctx, kv_local, heads),
        out_shape=jax.ShapeDtypeStruct((rows, kv_local * columns), jnp.bfloat16),
        in_specs=[vmem] * (kv_local + 1),
        out_specs=vmem,
        scratch_shapes=[
            pltpu.VMEM((chips, kv_local, rows, columns), jnp.bfloat16),
            pltpu.VMEM((chips, tall, rows), jnp.float32),
            pltpu.VMEM((chips, kv_local, rows, columns), jnp.bfloat16),
            pltpu.VMEM((chips, tall, rows), jnp.float32),
            pltpu.VMEM((fars, kv_local, rows, columns), jnp.bfloat16),
            pltpu.VMEM((fars, tall, rows), jnp.float32),
            pltpu.SemaphoreType.DMA((2, chips * (kv_local + 1))),
            pltpu.SemaphoreType.DMA((2, 2 * fars)),
        ],
        compiler_params=pltpu.CompilerParams(collective_id=1, has_side_effects=True, vmem_limit_bytes=40 * MIB),
        name="give_back",
    )(*parts, logs)


def body(join_states, query_weight, out_weight, outline_keys, outline_values, branch_keys, branch_values, branch_lengths, visibility):
    width = outline_keys.shape[2]
    head_count = query_weight.shape[1] // width
    group = head_count * lax.axis_size("head") // outline_keys.shape[0]
    kv_local = max(1, head_count // group)
    per_kv = head_count // kv_local
    kv_start = lax.axis_index("head") * head_count // group
    rows = join_states.shape[0]
    n_ctx = lax.axis_size("ctx")
    me = lax.axis_index("ctx")
    first = outline_keys.shape[1] * n_ctx + branch_keys.shape[1] + me * rows
    cosine, sine = rope_tables(rows, width, first, width ** (-0.5) * LOG2E)
    columns = per_kv * width
    gathered = []
    for kv in range(kv_local):
        queries = jnp.dot(join_states, query_weight[:, kv * columns:(kv + 1) * columns], preferred_element_type=jnp.float32)
        queries = queries.reshape(rows, per_kv, width)
        turned = jnp.concatenate([queries[..., width // 2:], queries[..., :width // 2]], axis=-1)
        rotated = (queries * cosine[:, None, :] + turned * sine[:, None, :]).astype(jnp.bfloat16)
        gathered.append(lax.all_gather(rotated.reshape(rows, columns), "ctx", axis=0, tiled=True))
    parts, logs = [], []
    for kv in range(kv_local):
        part, log = attend(gathered[kv], kv_start + kv, me, branch_lengths, visibility,
                           outline_keys, outline_values, branch_keys, branch_values)
        parts.append(part)
        logs.append(log)
    logs = jnp.concatenate(logs, axis=1)
    logs = jnp.pad(logs, ((0, 0), (0, -head_count % 8))).reshape(n_ctx, rows, -1).transpose(0, 2, 1)
    mixed = give_back(parts, logs, n_ctx, head_count)
    partial_out = jnp.dot(mixed, out_weight, preferred_element_type=jnp.float32)
    return lax.psum_scatter(partial_out.astype(jnp.bfloat16), "head", scatter_dimension=1, tiled=True)


def solution(mesh):
    return jax.shard_map(
        body,
        mesh=mesh,
        in_specs=(P("ctx", None), P(None, "head"), P("head", None), P(None, "ctx", None), P(None, "ctx", None),
                  P(None, "ctx", None), P(None, "ctx", None), P(), P()),
        out_specs=P("ctx", "head"),
        check_vma=False,
    )
```

```python
import functools

import jax
import jax.numpy as jnp
from jax import lax
from jax.experimental import pallas as pl
from jax.experimental.pallas import tpu as pltpu
from jax.sharding import PartitionSpec as P

JSPAN = 32
ROPE_BASE = 500000.0
LOG2E = 1.4426950408889634
HIDE = 1e30
CHUNK = 512
CHAINS = 2
SHARES = 2
MIB = 1 << 20


def rope_tables(rows, width, first, scale):
    half = width // 2
    freq = ROPE_BASE ** (-(jnp.arange(half, dtype=jnp.float32) * 2.0) / width)
    place = (first + jnp.arange(rows)).astype(jnp.float32)
    angle = place[:, None] * freq[None, :]
    cosine = jnp.cos(angle) * scale
    sine = jnp.sin(angle) * scale
    return jnp.concatenate([cosine, cosine], axis=1), jnp.concatenate([-sine, sine], axis=1)


def attend_kernel(per_kv, blocks_each, share, shares, n_ctx, at_ref, lengths_ref, seen_ref, q_ref, ok_ref, ov_ref, bk_ref, bv_ref,
                  o_ref, stat_ref, ov_wide, bv_wide, order):
    width = ok_ref.shape[2]
    me = at_ref[1]
    length = lengths_ref[me]
    blocks = q_ref.shape[0] // JSPAN
    each = blocks // n_ctx
    branch_most = bk_ref.shape[1]
    chunk = min(CHUNK, branch_most)
    ov_wide[:, :width] = ov_ref[0]
    ov_wide[:, width:] = jnp.ones((ov_ref.shape[1], width), jnp.bfloat16)
    bv_wide[:, :width] = bv_ref[0]
    bv_wide[:, width:] = jnp.ones((branch_most, width), jnp.bfloat16)

    def place(block, ends):
        front, back = ends
        hit = seen_ref[(block // each) * (each * shares) + share * each + block % each, me] == 1
        order[jnp.where(hit, front, back)] = block
        step = hit.astype(jnp.int32)
        return front + step, back - 1 + step

    seen_count, _ = lax.fori_loop(0, blocks, place, (jnp.int32(0), jnp.int32(blocks - 1)))

    def scores(query, keys):
        return lax.dot_general(query, keys, (((1,), (1,)), ((), ())), preferred_element_type=jnp.float32)

    tile = blocks_each * JSPAN
    per_turn = CHAINS * blocks_each

    def turn(step, _):
        base = step * per_turn
        starts, queries, states, shown = [], [], [], []
        row = lax.broadcasted_iota(jnp.int32, (per_kv * tile, 1), 0)
        slot = (row // JSPAN) % blocks_each
        for chain in range(CHAINS):
            first = base + chain * blocks_each
            at = [pl.multiple_of(order[first + j] * JSPAN, JSPAN) for j in range(blocks_each)]
            starts.append(at)
            queries.append(jnp.concatenate(
                [q_ref[pl.ds(at[j], JSPAN), h * width:(h + 1) * width] for h in range(per_kv) for j in range(blocks_each)],
                axis=0))
            shown.append(first + slot < seen_count)
        for chain in range(CHAINS):
            s = scores(queries[chain], ok_ref[0])
            best = jnp.max(s, axis=1, keepdims=True)
            weights = jnp.exp2((s - best).astype(jnp.bfloat16))
            states += [best, jnp.dot(weights, ov_wide[...], preferred_element_type=jnp.float32)]

        def more(part, state):
            begin = pl.multiple_of(part * chunk, chunk)
            keys = bk_ref[0, pl.ds(begin, chunk), :]
            values = bv_wide[pl.ds(begin, chunk), :]
            place_in = begin + lax.broadcasted_iota(jnp.int32, (1, chunk), 1)
            bias = jnp.where(place_in < length, 0.0, -HIDE)
            out = []
            for chain in range(CHAINS):
                best, acc = state[2 * chain], state[2 * chain + 1]
                s = scores(queries[chain], keys) + bias
                grown = jnp.maximum(best, jnp.max(s, axis=1, keepdims=True))
                new_best = jnp.where(shown[chain], grown, best)
                weights = jnp.exp2((s - jnp.where(shown[chain], grown, HIDE)).astype(jnp.bfloat16))
                acc = acc * jnp.exp2(best - new_best) + jnp.dot(weights, values, preferred_element_type=jnp.float32)
                out += [new_best, acc]
            return tuple(out)

        parts = jnp.where(base < seen_count, (length + chunk - 1) // chunk, 0)
        states = lax.fori_loop(0, parts, more, tuple(states))
        for chain in range(CHAINS):
            best, acc = states[2 * chain], states[2 * chain + 1]
            total = acc[:, width:]
            part_out = (acc[:, :width] / total).astype(o_ref.dtype)
            logs = best + jnp.log2(total[:, :1])
            for h in range(per_kv):
                for j in range(blocks_each):
                    here = (h * blocks_each + j) * JSPAN
                    rows = pl.ds(starts[chain][j], JSPAN)
                    o_ref[rows, h * width:(h + 1) * width] = part_out[here:here + JSPAN]
                    stat_ref[0, rows, h:h + 1] = logs[here:here + JSPAN]
        return 0

    lax.fori_loop(0, blocks // per_turn, turn, 0)


def attend(query, share, shares, n_ctx, kv_local, kv, me, lengths, seen, outline_keys, outline_values, branch_keys, branch_values):
    rows, columns = query.shape
    width = outline_keys.shape[2]
    per_kv = columns // (width * kv_local)
    outline_here, branch_most = outline_keys.shape[1], branch_keys.shape[1]
    mine = lambda i, at, lens, vis: (0, i)
    one = lambda i, at, lens, vis: (at[0] + i, 0, 0)
    keys_all = outline_here + branch_most // 2
    return pl.pallas_call(
        functools.partial(attend_kernel, per_kv, 2, share, shares, n_ctx),
        out_shape=(jax.ShapeDtypeStruct((rows, columns), jnp.bfloat16), jax.ShapeDtypeStruct((kv_local, rows, per_kv), jnp.float32)),
        grid_spec=pltpu.PrefetchScalarGridSpec(
            num_scalar_prefetch=3,
            grid=(kv_local,),
            in_specs=[
                pl.BlockSpec((rows, per_kv * width), mine),
                pl.BlockSpec((1, outline_here, width), one),
                pl.BlockSpec((1, outline_here, width), one),
                pl.BlockSpec((1, branch_most, width), one),
                pl.BlockSpec((1, branch_most, width), one),
            ],
            out_specs=(pl.BlockSpec((rows, per_kv * width), mine), pl.BlockSpec((1, rows, per_kv), lambda i, at, lens, vis: (i, 0, 0))),
            scratch_shapes=[
                pltpu.VMEM((outline_here, 2 * width), jnp.bfloat16),
                pltpu.VMEM((branch_most, 2 * width), jnp.bfloat16),
                pltpu.SMEM((rows // JSPAN,), jnp.int32),
            ],
        ),
        compiler_params=pltpu.CompilerParams(vmem_limit_bytes=60 * MIB),
        cost_estimate=pl.CostEstimate(
            flops=rows * columns * keys_all * 8, bytes_accessed=4 * rows * columns, transcendentals=rows * per_kv * kv_local * keys_all),
        name="attend",
    )(jnp.stack([kv, me]).astype(jnp.int32), lengths, seen, query, outline_keys, outline_values, branch_keys, branch_values)


def return_kernel(n_ctx, kv_local, heads, *refs):
    parts = refs[:kv_local]
    logs_ref, mixed_ref, near, near_logs, joined, joined_logs, far, far_logs = refs[kv_local:kv_local + 8]
    near_sems, far_sems = refs[kv_local + 8:]
    rows, columns = near.shape[2:]
    width = kv_local * columns // heads
    per_kv = columns // width
    chips = n_ctx // 2
    me = lax.axis_index("ctx")
    chip, core = me // 2, me % 2
    sibling = chip * 2 + 1 - core

    def peer(j):
        return ((chip + j) % chips) * 2

    def copy(src, dst, sems, which, device):
        return pltpu.make_async_remote_copy(
            src_ref=src, dst_ref=dst, send_sem=sems.at[0, which], recv_sem=sems.at[1, which],
            device_id={"ctx": device}, device_id_type=pl.DeviceIdType.MESH)

    barrier = pltpu.get_barrier_semaphore()
    pl.semaphore_signal(barrier, inc=1, device_id={"ctx": sibling}, device_id_type=pl.DeviceIdType.MESH)
    for j in range(1, chips):
        pl.semaphore_signal(barrier, inc=1, device_id={"ctx": peer(j) + core}, device_id_type=pl.DeviceIdType.MESH)
    pl.semaphore_wait(barrier, chips)

    def spread(shares):
        filled = jnp.concatenate([shares, jnp.zeros((128 - shares.shape[0], rows), jnp.float32)], axis=0)
        return filled.T

    sequence = [(j + 1) % chips for j in range(chips)]
    sequence = sequence[::-1][1:] + [0] if chips > 1 else sequence
    near_copies = {}
    for j in sequence:
        block = peer(j) + 1 - core
        mine = pl.ds(pl.multiple_of(block * rows, rows), rows)
        group = [copy(logs_ref.at[block], near_logs.at[j], near_sems, j * (kv_local + 1) + kv_local, sibling)]
        for kv in range(kv_local):
            group.append(copy(parts[kv].at[mine], near.at[j, kv], near_sems, j * (kv_local + 1) + kv, sibling))
        for c in group:
            c.start()
        near_copies[j] = group
    far_copies = {}
    for j in sequence:
        for c in near_copies[j]:
            c.wait_recv()
        block = peer(j) + core
        own, other = logs_ref[block], near_logs[j]
        top = jnp.maximum(own, other)
        own_share, other_share = jnp.exp2(own - top), jnp.exp2(other - top)
        total = own_share + other_share
        joined_logs[j] = top + jnp.log2(total)
        own_wide, other_wide = spread(own_share / total), spread(other_share / total)
        mine = pl.ds(pl.multiple_of(block * rows, rows), rows)
        for kv in range(kv_local):
            for h in range(per_kv):
                at, head = slice(h * width, (h + 1) * width), kv * per_kv + h
                value = (parts[kv][mine, at].astype(jnp.float32) * own_wide[:, head:head + 1]
                         + near[j, kv, :, at].astype(jnp.float32) * other_wide[:, head:head + 1])
                joined[j, kv, :, at] = value.astype(jnp.bfloat16)
        if j > 0:
            group = [copy(joined_logs.at[j], far_logs.at[j - 1], far_sems, 2 * (j - 1) + 1, peer(j) + core),
                     copy(joined.at[j], far.at[j - 1], far_sems, 2 * (j - 1), peer(j) + core)]
            for c in group:
                c.start()
            far_copies[j] = group
    for j in range(1, chips):
        for c in far_copies[j]:
            c.wait_recv()
    every = [joined_logs[0]] + [far_logs[j] for j in range(chips - 1)]
    top = functools.reduce(jnp.maximum, every)
    shares = [jnp.exp2(x - top) for x in every]
    total = functools.reduce(jnp.add, shares)
    wide = [spread(x / total) for x in shares]
    for kv in range(kv_local):
        for h in range(per_kv):
            at, head = slice(h * width, (h + 1) * width), kv * per_kv + h
            value = joined[0, kv, :, at].astype(jnp.float32) * wide[0][:, head:head + 1]
            for j in range(chips - 1):
                value += far[j, kv, :, at].astype(jnp.float32) * wide[j + 1][:, head:head + 1]
            mixed_ref[:, head * width:(head + 1) * width] = value.astype(jnp.bfloat16)
    for j in sequence:
        for c in near_copies[j] + far_copies.get(j, []):
            c.wait_send()


def give_back(parts, logs, n_ctx, heads, number):
    kv_local = len(parts)
    rows, columns = parts[0].shape[0] // n_ctx, parts[0].shape[1]
    chips = n_ctx // 2
    fars = max(chips - 1, 1)
    tall = logs.shape[1]
    vmem = pl.BlockSpec(memory_space=pltpu.VMEM)
    return pl.pallas_call(
        functools.partial(return_kernel, n_ctx, kv_local, heads),
        out_shape=jax.ShapeDtypeStruct((rows, kv_local * columns), jnp.bfloat16),
        in_specs=[vmem] * (kv_local + 1),
        out_specs=vmem,
        scratch_shapes=[
            pltpu.VMEM((chips, kv_local, rows, columns), jnp.bfloat16),
            pltpu.VMEM((chips, tall, rows), jnp.float32),
            pltpu.VMEM((chips, kv_local, rows, columns), jnp.bfloat16),
            pltpu.VMEM((chips, tall, rows), jnp.float32),
            pltpu.VMEM((fars, kv_local, rows, columns), jnp.bfloat16),
            pltpu.VMEM((fars, tall, rows), jnp.float32),
            pltpu.SemaphoreType.DMA((2, chips * (kv_local + 1))),
            pltpu.SemaphoreType.DMA((2, 2 * fars)),
        ],
        compiler_params=pltpu.CompilerParams(collective_id=number, has_side_effects=True, vmem_limit_bytes=40 * MIB),
        name="give_back",
    )(*parts, logs)


def body(join_states, query_weight, out_weight, outline_keys, outline_values, branch_keys, branch_values, branch_lengths, visibility):
    width = outline_keys.shape[2]
    head_count = query_weight.shape[1] // width
    group = head_count * lax.axis_size("head") // outline_keys.shape[0]
    kv_local = max(1, head_count // group)
    per_kv = head_count // kv_local
    kv_start = lax.axis_index("head") * head_count // group
    rows = join_states.shape[0]
    n_ctx = lax.axis_size("ctx")
    me = lax.axis_index("ctx")
    first = outline_keys.shape[1] * n_ctx + branch_keys.shape[1] + me * rows
    cosine, sine = rope_tables(rows, width, first, width ** (-0.5) * LOG2E)
    shares = SHARES
    some = rows // shares
    gathered = []
    for share in range(shares):
        mine = slice(share * some, (share + 1) * some)
        queries = jnp.dot(join_states[mine], query_weight, preferred_element_type=jnp.float32)
        queries = queries.reshape(some, head_count, width)
        turned = jnp.concatenate([queries[..., width // 2:], queries[..., :width // 2]], axis=-1)
        rotated = (queries * cosine[mine, None, :] + turned * sine[mine, None, :]).astype(jnp.bfloat16)
        gathered.append(lax.all_gather(rotated.reshape(some, head_count * width), "ctx", axis=0, tiled=True))
    outs = []
    partial_out = None
    for share in range(shares):
        query = gathered[share]
        if share > 0:
            query, partial_out = lax.optimization_barrier((query, partial_out))
            outs.append(lax.psum_scatter(partial_out, "head", scatter_dimension=1, tiled=True))
        part, logs = attend(query, share, shares, n_ctx, kv_local, kv_start, me, branch_lengths, visibility,
                            outline_keys, outline_values, branch_keys, branch_values)
        if share > 0:
            part, outs[-1] = lax.optimization_barrier((part, outs[-1]))
        logs = logs.reshape(kv_local, n_ctx, some, per_kv).transpose(1, 0, 3, 2).reshape(n_ctx, head_count, some)
        logs = jnp.pad(logs, ((0, 0), (0, -head_count % 8), (0, 0)))
        mixed = give_back([part], logs, n_ctx, head_count, share + 1)
        partial_out = jnp.dot(mixed, out_weight, preferred_element_type=jnp.float32).astype(jnp.bfloat16)
    outs.append(lax.psum_scatter(partial_out, "head", scatter_dimension=1, tiled=True))
    return jnp.concatenate(outs, axis=0)


def solution(mesh):
    return jax.shard_map(
        body,
        mesh=mesh,
        in_specs=(P("ctx", None), P(None, "head"), P("head", None), P(None, "ctx", None), P(None, "ctx", None),
                  P(None, "ctx", None), P(None, "ctx", None), P(), P()),
        out_specs=P("ctx", "head"),
        check_vma=False,
    )
```

```python
import functools

import jax
import jax.numpy as jnp
from jax import lax
from jax.experimental import pallas as pl
from jax.experimental.pallas import tpu as pltpu
from jax.sharding import PartitionSpec as P

JSPAN = 32
ROPE_BASE = 500000.0
LOG2E = 1.4426950408889634
HIDE = 1e30
CHUNK = 512
SHARES = 2
MIB = 1 << 20


def rope_tables(rows, width, first, scale):
    half = width // 2
    freq = ROPE_BASE ** (-(jnp.arange(half, dtype=jnp.float32) * 2.0) / width)
    place = (first + jnp.arange(rows)).astype(jnp.float32)
    angle = place[:, None] * freq[None, :]
    cosine = jnp.cos(angle) * scale
    sine = jnp.sin(angle) * scale
    return jnp.concatenate([cosine, cosine], axis=1), jnp.concatenate([-sine, sine], axis=1)


def attend_kernel(per_kv, blocks_each, share, shares, n_ctx, at_ref, lengths_ref, seen_ref, q_ref, ok_ref, ov_ref, bk_ref, bv_ref,
                  o_ref, stat_ref, ok_turned, bk_turned, ov_wide, bv_wide, order):
    width = ok_ref.shape[2]
    me = at_ref[1]
    length = lengths_ref[me]
    blocks = q_ref.shape[0] // JSPAN
    each = blocks // n_ctx
    branch_most = bk_ref.shape[1]
    chunk = min(CHUNK, branch_most)
    ok_turned[...] = ok_ref[0].T
    for part in range(branch_most // chunk):
        bk_turned[part] = bk_ref[0, part * chunk:(part + 1) * chunk].T
    ov_wide[:, :width] = ov_ref[0]
    ov_wide[:, width:] = jnp.ones((ov_ref.shape[1], width), jnp.bfloat16)
    bv_wide[:, :width] = bv_ref[0]
    bv_wide[:, width:] = jnp.ones((branch_most, width), jnp.bfloat16)

    def place(block, ends):
        front, back = ends
        hit = seen_ref[(block // each) * (each * shares) + share * each + block % each, me] == 1
        order[jnp.where(hit, front, back)] = block
        step = hit.astype(jnp.int32)
        return front + step, back - 1 + step

    seen_count, _ = lax.fori_loop(0, blocks, place, (jnp.int32(0), jnp.int32(blocks - 1)))

    tile = blocks_each * JSPAN
    chunks = branch_most // chunk

    def turn(step, _):
        base = step * blocks_each
        starts = [pl.multiple_of(order[base + j] * JSPAN, JSPAN) for j in range(blocks_each)]

        def go(live):
            query = jnp.concatenate(
                [q_ref[pl.ds(at, JSPAN), h * width:(h + 1) * width] for h in range(per_kv) for at in starts], axis=0)
            s = jnp.dot(query, ok_turned[...], preferred_element_type=jnp.float32)
            best = jnp.max(s, axis=1, keepdims=True)
            lower = best
            found = []
            if live > 0:
                row = lax.broadcasted_iota(jnp.int32, (per_kv * tile, 1), 0)
                shown = (row & (tile - 1)) < (seen_count - base) * JSPAN
                for part in range(live):
                    more = jnp.dot(query, bk_turned[part], preferred_element_type=jnp.float32)
                    if part == live - 1:
                        place_in = part * chunk + lax.broadcasted_iota(jnp.int32, (1, chunk), 1)
                        more = more + jnp.where(place_in < length, 0.0, -HIDE)
                    found.append(more)
                grown = best
                for more in found:
                    grown = jnp.maximum(grown, jnp.max(more, axis=1, keepdims=True))
                best = jnp.where(shown, grown, best)
                lower = jnp.where(shown, grown, HIDE)
            acc = jnp.dot(jnp.exp2(s - best).astype(jnp.bfloat16), ov_wide[...], preferred_element_type=jnp.float32)
            for part, more in enumerate(found):
                weights = jnp.exp2(more - lower).astype(jnp.bfloat16)
                acc += jnp.dot(weights, bv_wide[part * chunk:(part + 1) * chunk], preferred_element_type=jnp.float32)
            total = acc[:, width:]
            part_out = (acc[:, :width] / total).astype(o_ref.dtype)
            logs = best + jnp.log2(total[:, :1])
            for h in range(per_kv):
                for j in range(blocks_each):
                    here = (h * blocks_each + j) * JSPAN
                    rows = pl.ds(starts[j], JSPAN)
                    o_ref[rows, h * width:(h + 1) * width] = part_out[here:here + JSPAN]
                    stat_ref[0, rows, h:h + 1] = logs[here:here + JSPAN]

        needed = jnp.where(base < seen_count, (length + chunk - 1) // chunk, 0)
        for live in range(chunks + 1):
            pl.when(needed == live)(functools.partial(go, live))
        return 0

    lax.fori_loop(0, blocks // blocks_each, turn, 0)


def attend(query, share, shares, n_ctx, kv_local, kv, me, lengths, seen, outline_keys, outline_values, branch_keys, branch_values):
    rows, columns = query.shape
    width = outline_keys.shape[2]
    per_kv = columns // (width * kv_local)
    outline_here, branch_most = outline_keys.shape[1], branch_keys.shape[1]
    mine = lambda i, at, lens, vis: (0, i)
    one = lambda i, at, lens, vis: (at[0] + i, 0, 0)
    keys_all = outline_here + branch_most // 2
    return pl.pallas_call(
        functools.partial(attend_kernel, per_kv, 4, share, shares, n_ctx),
        out_shape=(jax.ShapeDtypeStruct((rows, columns), jnp.bfloat16), jax.ShapeDtypeStruct((kv_local, rows, per_kv), jnp.float32)),
        grid_spec=pltpu.PrefetchScalarGridSpec(
            num_scalar_prefetch=3,
            grid=(kv_local,),
            in_specs=[
                pl.BlockSpec((rows, per_kv * width), mine),
                pl.BlockSpec((1, outline_here, width), one),
                pl.BlockSpec((1, outline_here, width), one),
                pl.BlockSpec((1, branch_most, width), one),
                pl.BlockSpec((1, branch_most, width), one),
            ],
            out_specs=(pl.BlockSpec((rows, per_kv * width), mine), pl.BlockSpec((1, rows, per_kv), lambda i, at, lens, vis: (i, 0, 0))),
            scratch_shapes=[
                pltpu.VMEM((width, outline_here), jnp.bfloat16),
                pltpu.VMEM((branch_most // min(CHUNK, branch_most), width, min(CHUNK, branch_most)), jnp.bfloat16),
                pltpu.VMEM((outline_here, 2 * width), jnp.bfloat16),
                pltpu.VMEM((branch_most, 2 * width), jnp.bfloat16),
                pltpu.SMEM((rows // JSPAN,), jnp.int32),
            ],
        ),
        compiler_params=pltpu.CompilerParams(vmem_limit_bytes=60 * MIB),
        cost_estimate=pl.CostEstimate(
            flops=rows * columns * keys_all * 8, bytes_accessed=4 * rows * columns, transcendentals=rows * per_kv * kv_local * keys_all),
        name="attend",
    )(jnp.stack([kv, me]).astype(jnp.int32), lengths, seen, query, outline_keys, outline_values, branch_keys, branch_values)


def return_kernel(n_ctx, kv_local, heads, *refs):
    parts = refs[:kv_local]
    logs_ref, mixed_ref, near, near_logs, joined, joined_logs, far, far_logs = refs[kv_local:kv_local + 8]
    near_sems, far_sems = refs[kv_local + 8:]
    rows, columns = near.shape[2:]
    width = kv_local * columns // heads
    per_kv = columns // width
    chips = n_ctx // 2
    me = lax.axis_index("ctx")
    chip, core = me // 2, me % 2
    sibling = chip * 2 + 1 - core

    def peer(j):
        return ((chip + j) % chips) * 2

    def copy(src, dst, sems, which, device):
        return pltpu.make_async_remote_copy(
            src_ref=src, dst_ref=dst, send_sem=sems.at[0, which], recv_sem=sems.at[1, which],
            device_id={"ctx": device}, device_id_type=pl.DeviceIdType.MESH)

    barrier = pltpu.get_barrier_semaphore()
    pl.semaphore_signal(barrier, inc=1, device_id={"ctx": sibling}, device_id_type=pl.DeviceIdType.MESH)
    for j in range(1, chips):
        pl.semaphore_signal(barrier, inc=1, device_id={"ctx": peer(j) + core}, device_id_type=pl.DeviceIdType.MESH)
    pl.semaphore_wait(barrier, chips)

    def spread(shares):
        filled = jnp.concatenate([shares, jnp.zeros((128 - shares.shape[0], rows), jnp.float32)], axis=0)
        return filled.T

    sequence = [(j + 1) % chips for j in range(chips)]
    sequence = sequence[::-1][1:] + [0] if chips > 1 else sequence
    near_copies = {}
    for j in sequence:
        block = peer(j) + 1 - core
        mine = pl.ds(pl.multiple_of(block * rows, rows), rows)
        group = [copy(logs_ref.at[block], near_logs.at[j], near_sems, j * (kv_local + 1) + kv_local, sibling)]
        for kv in range(kv_local):
            group.append(copy(parts[kv].at[mine], near.at[j, kv], near_sems, j * (kv_local + 1) + kv, sibling))
        for c in group:
            c.start()
        near_copies[j] = group
    far_copies = {}
    for j in sequence:
        for c in near_copies[j]:
            c.wait_recv()
        block = peer(j) + core
        own, other = logs_ref[block], near_logs[j]
        top = jnp.maximum(own, other)
        own_share, other_share = jnp.exp2(own - top), jnp.exp2(other - top)
        total = own_share + other_share
        joined_logs[j] = top + jnp.log2(total)
        own_wide, other_wide = spread(own_share / total), spread(other_share / total)
        mine = pl.ds(pl.multiple_of(block * rows, rows), rows)
        for kv in range(kv_local):
            for h in range(per_kv):
                at, head = slice(h * width, (h + 1) * width), kv * per_kv + h
                value = (parts[kv][mine, at].astype(jnp.float32) * own_wide[:, head:head + 1]
                         + near[j, kv, :, at].astype(jnp.float32) * other_wide[:, head:head + 1])
                joined[j, kv, :, at] = value.astype(jnp.bfloat16)
        if j > 0:
            group = [copy(joined_logs.at[j], far_logs.at[j - 1], far_sems, 2 * (j - 1) + 1, peer(j) + core),
                     copy(joined.at[j], far.at[j - 1], far_sems, 2 * (j - 1), peer(j) + core)]
            for c in group:
                c.start()
            far_copies[j] = group
    for j in range(1, chips):
        for c in far_copies[j]:
            c.wait_recv()
    every = [joined_logs[0]] + [far_logs[j] for j in range(chips - 1)]
    top = functools.reduce(jnp.maximum, every)
    shares = [jnp.exp2(x - top) for x in every]
    total = functools.reduce(jnp.add, shares)
    wide = [spread(x / total) for x in shares]
    for kv in range(kv_local):
        for h in range(per_kv):
            at, head = slice(h * width, (h + 1) * width), kv * per_kv + h
            value = joined[0, kv, :, at].astype(jnp.float32) * wide[0][:, head:head + 1]
            for j in range(chips - 1):
                value += far[j, kv, :, at].astype(jnp.float32) * wide[j + 1][:, head:head + 1]
            mixed_ref[:, head * width:(head + 1) * width] = value.astype(jnp.bfloat16)
    for j in sequence:
        for c in near_copies[j] + far_copies.get(j, []):
            c.wait_send()


def give_back(parts, logs, n_ctx, heads, number):
    kv_local = len(parts)
    rows, columns = parts[0].shape[0] // n_ctx, parts[0].shape[1]
    chips = n_ctx // 2
    fars = max(chips - 1, 1)
    tall = logs.shape[1]
    vmem = pl.BlockSpec(memory_space=pltpu.VMEM)
    return pl.pallas_call(
        functools.partial(return_kernel, n_ctx, kv_local, heads),
        out_shape=jax.ShapeDtypeStruct((rows, kv_local * columns), jnp.bfloat16),
        in_specs=[vmem] * (kv_local + 1),
        out_specs=vmem,
        scratch_shapes=[
            pltpu.VMEM((chips, kv_local, rows, columns), jnp.bfloat16),
            pltpu.VMEM((chips, tall, rows), jnp.float32),
            pltpu.VMEM((chips, kv_local, rows, columns), jnp.bfloat16),
            pltpu.VMEM((chips, tall, rows), jnp.float32),
            pltpu.VMEM((fars, kv_local, rows, columns), jnp.bfloat16),
            pltpu.VMEM((fars, tall, rows), jnp.float32),
            pltpu.SemaphoreType.DMA((2, chips * (kv_local + 1))),
            pltpu.SemaphoreType.DMA((2, 2 * fars)),
        ],
        compiler_params=pltpu.CompilerParams(collective_id=number, has_side_effects=True, vmem_limit_bytes=40 * MIB),
        name="give_back",
    )(*parts, logs)


def body(join_states, query_weight, out_weight, outline_keys, outline_values, branch_keys, branch_values, branch_lengths, visibility):
    width = outline_keys.shape[2]
    head_count = query_weight.shape[1] // width
    group = head_count * lax.axis_size("head") // outline_keys.shape[0]
    kv_local = max(1, head_count // group)
    per_kv = head_count // kv_local
    kv_start = lax.axis_index("head") * head_count // group
    rows = join_states.shape[0]
    n_ctx = lax.axis_size("ctx")
    me = lax.axis_index("ctx")
    first = outline_keys.shape[1] * n_ctx + branch_keys.shape[1] + me * rows
    cosine, sine = rope_tables(rows, width, first, width ** (-0.5) * LOG2E)
    shares = SHARES
    some = rows // shares
    gathered = []
    for share in range(shares):
        mine = slice(share * some, (share + 1) * some)
        queries = jnp.dot(join_states[mine], query_weight, preferred_element_type=jnp.float32)
        queries = queries.reshape(some, head_count, width)
        turned = jnp.concatenate([queries[..., width // 2:], queries[..., :width // 2]], axis=-1)
        rotated = (queries * cosine[mine, None, :] + turned * sine[mine, None, :]).astype(jnp.bfloat16)
        gathered.append(lax.all_gather(rotated.reshape(some, head_count * width), "ctx", axis=0, tiled=True))
    outs = []
    partial_out = None
    for share in range(shares):
        query = gathered[share]
        if share > 0:
            query, partial_out = lax.optimization_barrier((query, partial_out))
            outs.append(lax.psum_scatter(partial_out, "head", scatter_dimension=1, tiled=True))
        part, logs = attend(query, share, shares, n_ctx, kv_local, kv_start, me, branch_lengths, visibility,
                            outline_keys, outline_values, branch_keys, branch_values)
        if share > 0:
            part, outs[-1] = lax.optimization_barrier((part, outs[-1]))
        logs = logs.reshape(kv_local, n_ctx, some, per_kv).transpose(1, 0, 3, 2).reshape(n_ctx, head_count, some)
        logs = jnp.pad(logs, ((0, 0), (0, -head_count % 8), (0, 0)))
        mixed = give_back([part], logs, n_ctx, head_count, share + 1)
        partial_out = jnp.dot(mixed, out_weight, preferred_element_type=jnp.float32).astype(jnp.bfloat16)
    outs.append(lax.psum_scatter(partial_out, "head", scatter_dimension=1, tiled=True))
    return jnp.concatenate(outs, axis=0)


def solution(mesh):
    return jax.shard_map(
        body,
        mesh=mesh,
        in_specs=(P("ctx", None), P(None, "head"), P("head", None), P(None, "ctx", None), P(None, "ctx", None),
                  P(None, "ctx", None), P(None, "ctx", None), P(), P()),
        out_specs=P("ctx", "head"),
        check_vma=False,
    )
```

```python
import functools

import jax
import jax.numpy as jnp
from jax import lax
from jax.experimental import pallas as pl
from jax.experimental.pallas import tpu as pltpu
from jax.sharding import PartitionSpec as P

JSPAN = 32
ROPE_BASE = 500000.0
LOG2E = 1.4426950408889634
HIDE = 1e30
CHUNK = 512
SHARES = 2
MIB = 1 << 20


def rope_tables(rows, width, first, scale):
    half = width // 2
    freq = ROPE_BASE ** (-(jnp.arange(half, dtype=jnp.float32) * 2.0) / width)
    place = (first + jnp.arange(rows)).astype(jnp.float32)
    angle = place[:, None] * freq[None, :]
    cosine = jnp.cos(angle) * scale
    sine = jnp.sin(angle) * scale
    return jnp.concatenate([cosine, cosine], axis=1), jnp.concatenate([-sine, sine], axis=1)


def attend_kernel(per_kv, blocks_each, share, shares, n_ctx, at_ref, lengths_ref, seen_ref, q_ref, ok_ref, ov_ref, bk_ref, bv_ref,
                  o_ref, stat_ref, ok_turned, bk_turned, ov_wide, bv_wide, order):
    width = ok_ref.shape[2]
    me = at_ref[1]
    length = lengths_ref[me]
    blocks = q_ref.shape[0] // JSPAN
    each = blocks // n_ctx
    branch_most = bk_ref.shape[1]
    chunk = min(CHUNK, branch_most)
    ok_turned[...] = ok_ref[0].T
    for part in range(branch_most // chunk):
        bk_turned[part] = bk_ref[0, part * chunk:(part + 1) * chunk].T
    ov_wide[:, :width] = ov_ref[0]
    ov_wide[:, width:] = jnp.ones((ov_ref.shape[1], width), jnp.bfloat16)
    bv_wide[:, :width] = bv_ref[0]
    bv_wide[:, width:] = jnp.ones((branch_most, width), jnp.bfloat16)

    def place(block, ends):
        front, back = ends
        hit = seen_ref[(block // each) * (each * shares) + share * each + block % each, me] == 1
        order[jnp.where(hit, front, back)] = block
        step = hit.astype(jnp.int32)
        return front + step, back - 1 + step

    seen_count, _ = lax.fori_loop(0, blocks, place, (jnp.int32(0), jnp.int32(blocks - 1)))

    tile = blocks_each * JSPAN
    chunks = branch_most // chunk

    def turn(step, _):
        base = step * blocks_each
        starts = [pl.multiple_of(order[base + j] * JSPAN, JSPAN) for j in range(blocks_each)]

        def go(live):
            query = jnp.concatenate(
                [q_ref[pl.ds(at, JSPAN), h * width:(h + 1) * width] for h in range(per_kv) for at in starts], axis=0)
            s = jnp.dot(query, ok_turned[...], preferred_element_type=jnp.float32)
            best = jnp.max(s, axis=1, keepdims=True)
            lower = best
            found = []
            if live > 0:
                row = lax.broadcasted_iota(jnp.int32, (per_kv * tile, 1), 0)
                shown = (row & (tile - 1)) < (seen_count - base) * JSPAN
                for part in range(live):
                    more = jnp.dot(query, bk_turned[part], preferred_element_type=jnp.float32)
                    if part == live - 1:
                        place_in = part * chunk + lax.broadcasted_iota(jnp.int32, (1, chunk), 1)
                        more = more + jnp.where(place_in < length, 0.0, -HIDE)
                    found.append(more)
                grown = best
                for more in found:
                    grown = jnp.maximum(grown, jnp.max(more, axis=1, keepdims=True))
                best = jnp.where(shown, grown, best)
                lower = jnp.where(shown, grown, HIDE)
            acc = jnp.dot(jnp.exp2(s - best).astype(jnp.bfloat16), ov_wide[...], preferred_element_type=jnp.float32)
            for part, more in enumerate(found):
                weights = jnp.exp2(more - lower).astype(jnp.bfloat16)
                acc += jnp.dot(weights, bv_wide[part * chunk:(part + 1) * chunk], preferred_element_type=jnp.float32)
            total = acc[:, width:]
            part_out = (acc[:, :width] / total).astype(o_ref.dtype)
            logs = best + jnp.log2(total[:, :1])
            for h in range(per_kv):
                for j in range(blocks_each):
                    here = (h * blocks_each + j) * JSPAN
                    rows = pl.ds(starts[j], JSPAN)
                    o_ref[rows, h * width:(h + 1) * width] = part_out[here:here + JSPAN]
                    stat_ref[0, rows, h:h + 1] = logs[here:here + JSPAN]

        needed = jnp.where(base < seen_count, (length + chunk - 1) // chunk, 0)
        for live in range(chunks + 1):
            pl.when(needed == live)(functools.partial(go, live))
        return 0

    lax.fori_loop(0, blocks // blocks_each, turn, 0)


def attend(query, share, shares, n_ctx, kv_local, kv, me, lengths, seen, outline_keys, outline_values, branch_keys, branch_values):
    rows, columns = query.shape
    width = outline_keys.shape[2]
    per_kv = columns // (width * kv_local)
    outline_here, branch_most = outline_keys.shape[1], branch_keys.shape[1]
    mine = lambda i, at, lens, vis: (0, i)
    one = lambda i, at, lens, vis: (at[0] + i, 0, 0)
    keys_all = outline_here + branch_most // 2
    return pl.pallas_call(
        functools.partial(attend_kernel, per_kv, 4, share, shares, n_ctx),
        out_shape=(jax.ShapeDtypeStruct((rows, columns), jnp.bfloat16), jax.ShapeDtypeStruct((kv_local, rows, per_kv), jnp.float32)),
        grid_spec=pltpu.PrefetchScalarGridSpec(
            num_scalar_prefetch=3,
            grid=(kv_local,),
            in_specs=[
                pl.BlockSpec((rows, per_kv * width), mine),
                pl.BlockSpec((1, outline_here, width), one),
                pl.BlockSpec((1, outline_here, width), one),
                pl.BlockSpec((1, branch_most, width), one),
                pl.BlockSpec((1, branch_most, width), one),
            ],
            out_specs=(pl.BlockSpec((rows, per_kv * width), mine), pl.BlockSpec((1, rows, per_kv), lambda i, at, lens, vis: (i, 0, 0))),
            scratch_shapes=[
                pltpu.VMEM((width, outline_here), jnp.bfloat16),
                pltpu.VMEM((branch_most // min(CHUNK, branch_most), width, min(CHUNK, branch_most)), jnp.bfloat16),
                pltpu.VMEM((outline_here, 2 * width), jnp.bfloat16),
                pltpu.VMEM((branch_most, 2 * width), jnp.bfloat16),
                pltpu.SMEM((rows // JSPAN,), jnp.int32),
            ],
        ),
        compiler_params=pltpu.CompilerParams(vmem_limit_bytes=60 * MIB),
        cost_estimate=pl.CostEstimate(
            flops=rows * columns * keys_all * 8, bytes_accessed=4 * rows * columns, transcendentals=rows * per_kv * kv_local * keys_all),
        name="attend",
    )(jnp.stack([kv, me]).astype(jnp.int32), lengths, seen, query, outline_keys, outline_values, branch_keys, branch_values)


def return_kernel(n_ctx, kv_local, heads, *refs):
    parts = refs[:kv_local]
    logs_ref, mixed_ref, near, near_logs, joined, joined_logs, far, far_logs, own_part = refs[kv_local:kv_local + 9]
    near_sems, far_sems, own_sems = refs[kv_local + 9:]
    rows, columns = near.shape[2:]
    width = kv_local * columns // heads
    per_kv = columns // width
    chips = n_ctx // 2
    me = lax.axis_index("ctx")
    chip, core = me // 2, me % 2
    sibling = chip * 2 + 1 - core

    def peer(j):
        return ((chip + j) % chips) * 2

    def copy(src, dst, sems, which, device):
        return pltpu.make_async_remote_copy(
            src_ref=src, dst_ref=dst, send_sem=sems.at[0, which], recv_sem=sems.at[1, which],
            device_id={"ctx": device}, device_id_type=pl.DeviceIdType.MESH)

    barrier = pltpu.get_barrier_semaphore()
    pl.semaphore_signal(barrier, inc=1, device_id={"ctx": sibling}, device_id_type=pl.DeviceIdType.MESH)
    for j in range(1, chips):
        pl.semaphore_signal(barrier, inc=1, device_id={"ctx": peer(j) + core}, device_id_type=pl.DeviceIdType.MESH)
    pl.semaphore_wait(barrier, chips)

    def spread(shares):
        filled = jnp.concatenate([shares, jnp.zeros((128 - shares.shape[0], rows), jnp.float32)], axis=0)
        return filled.T

    sequence = [(j + 1) % chips for j in range(chips)]
    sequence = sequence[::-1][1:] + [0] if chips > 1 else sequence
    own_copies = {}
    for j in sequence:
        mine = pl.ds(pl.multiple_of((peer(j) + core) * rows, rows), rows)
        own_copies[j] = [pltpu.make_async_copy(parts[kv].at[mine], own_part.at[j, kv], own_sems.at[j * kv_local + kv])
                         for kv in range(kv_local)]
    near_copies = {}
    for j in sequence:
        block = peer(j) + 1 - core
        mine = pl.ds(pl.multiple_of(block * rows, rows), rows)
        group = [copy(logs_ref.at[block], near_logs.at[j], near_sems, j * (kv_local + 1) + kv_local, sibling)]
        for kv in range(kv_local):
            group.append(copy(parts[kv].at[mine], near.at[j, kv], near_sems, j * (kv_local + 1) + kv, sibling))
        for c in group + own_copies[j]:
            c.start()
        near_copies[j] = group
    far_copies = {}
    for j in sequence:
        for c in own_copies[j]:
            c.wait()
        for c in near_copies[j]:
            c.wait_recv()
        block = peer(j) + core
        own, other = logs_ref[block], near_logs[j]
        top = jnp.maximum(own, other)
        own_share, other_share = jnp.exp2(own - top), jnp.exp2(other - top)
        total = own_share + other_share
        joined_logs[j] = top + jnp.log2(total)
        own_wide, other_wide = spread(own_share / total), spread(other_share / total)
        for kv in range(kv_local):
            for h in range(per_kv):
                at, head = slice(h * width, (h + 1) * width), kv * per_kv + h
                value = (own_part[j, kv, :, at].astype(jnp.float32) * own_wide[:, head:head + 1]
                         + near[j, kv, :, at].astype(jnp.float32) * other_wide[:, head:head + 1])
                joined[j, kv, :, at] = value.astype(jnp.bfloat16)
        if j > 0:
            group = [copy(joined_logs.at[j], far_logs.at[j - 1], far_sems, 2 * (j - 1) + 1, peer(j) + core),
                     copy(joined.at[j], far.at[j - 1], far_sems, 2 * (j - 1), peer(j) + core)]
            for c in group:
                c.start()
            far_copies[j] = group
    for j in range(1, chips):
        for c in far_copies[j]:
            c.wait_recv()
    every = [joined_logs[0]] + [far_logs[j] for j in range(chips - 1)]
    top = functools.reduce(jnp.maximum, every)
    shares = [jnp.exp2(x - top) for x in every]
    total = functools.reduce(jnp.add, shares)
    wide = [spread(x / total) for x in shares]
    for kv in range(kv_local):
        for h in range(per_kv):
            at, head = slice(h * width, (h + 1) * width), kv * per_kv + h
            value = joined[0, kv, :, at].astype(jnp.float32) * wide[0][:, head:head + 1]
            for j in range(chips - 1):
                value += far[j, kv, :, at].astype(jnp.float32) * wide[j + 1][:, head:head + 1]
            mixed_ref[:, head * width:(head + 1) * width] = value.astype(jnp.bfloat16)
    for j in sequence:
        for c in near_copies[j] + far_copies.get(j, []):
            c.wait_send()


def give_back(parts, logs, n_ctx, heads, number):
    kv_local = len(parts)
    rows, columns = parts[0].shape[0] // n_ctx, parts[0].shape[1]
    chips = n_ctx // 2
    fars = max(chips - 1, 1)
    tall = logs.shape[1]
    vmem = pl.BlockSpec(memory_space=pltpu.VMEM)
    return pl.pallas_call(
        functools.partial(return_kernel, n_ctx, kv_local, heads),
        out_shape=jax.ShapeDtypeStruct((rows, kv_local * columns), jnp.bfloat16),
        in_specs=[pl.BlockSpec(memory_space=pl.ANY)] * kv_local + [vmem],
        out_specs=vmem,
        scratch_shapes=[
            pltpu.VMEM((chips, kv_local, rows, columns), jnp.bfloat16),
            pltpu.VMEM((chips, tall, rows), jnp.float32),
            pltpu.VMEM((chips, kv_local, rows, columns), jnp.bfloat16),
            pltpu.VMEM((chips, tall, rows), jnp.float32),
            pltpu.VMEM((fars, kv_local, rows, columns), jnp.bfloat16),
            pltpu.VMEM((fars, tall, rows), jnp.float32),
            pltpu.VMEM((chips, kv_local, rows, columns), jnp.bfloat16),
            pltpu.SemaphoreType.DMA((2, chips * (kv_local + 1))),
            pltpu.SemaphoreType.DMA((2, 2 * fars)),
            pltpu.SemaphoreType.DMA((chips * kv_local,)),
        ],
        compiler_params=pltpu.CompilerParams(collective_id=number, has_side_effects=True, vmem_limit_bytes=60 * MIB),
        name="give_back",
    )(*parts, logs)


def body(join_states, query_weight, out_weight, outline_keys, outline_values, branch_keys, branch_values, branch_lengths, visibility):
    width = outline_keys.shape[2]
    head_count = query_weight.shape[1] // width
    group = head_count * lax.axis_size("head") // outline_keys.shape[0]
    kv_local = max(1, head_count // group)
    per_kv = head_count // kv_local
    kv_start = lax.axis_index("head") * head_count // group
    rows = join_states.shape[0]
    n_ctx = lax.axis_size("ctx")
    me = lax.axis_index("ctx")
    first = outline_keys.shape[1] * n_ctx + branch_keys.shape[1] + me * rows
    cosine, sine = rope_tables(rows, width, first, width ** (-0.5) * LOG2E)
    shares = SHARES
    some = rows // shares
    gathered = []
    for share in range(shares):
        mine = slice(share * some, (share + 1) * some)
        queries = jnp.dot(join_states[mine], query_weight, preferred_element_type=jnp.float32)
        queries = queries.reshape(some, head_count, width)
        turned = jnp.concatenate([queries[..., width // 2:], queries[..., :width // 2]], axis=-1)
        rotated = (queries * cosine[mine, None, :] + turned * sine[mine, None, :]).astype(jnp.bfloat16)
        gathered.append(lax.all_gather(rotated.reshape(some, head_count * width), "ctx", axis=0, tiled=True))
    outs = []
    partial_out = None
    for share in range(shares):
        query = gathered[share]
        if share > 0:
            query, partial_out = lax.optimization_barrier((query, partial_out))
            outs.append(lax.psum_scatter(partial_out, "head", scatter_dimension=1, tiled=True))
        part, logs = attend(query, share, shares, n_ctx, kv_local, kv_start, me, branch_lengths, visibility,
                            outline_keys, outline_values, branch_keys, branch_values)
        if share > 0:
            part, outs[-1] = lax.optimization_barrier((part, outs[-1]))
        logs = logs.reshape(kv_local, n_ctx, some, per_kv).transpose(1, 0, 3, 2).reshape(n_ctx, head_count, some)
        logs = jnp.pad(logs, ((0, 0), (0, -head_count % 8), (0, 0)))
        mixed = give_back([part], logs, n_ctx, head_count, share + 1)
        partial_out = jnp.dot(mixed, out_weight, preferred_element_type=jnp.float32).astype(jnp.bfloat16)
    outs.append(lax.psum_scatter(partial_out, "head", scatter_dimension=1, tiled=True))
    return jnp.concatenate(outs, axis=0)


def solution(mesh):
    return jax.shard_map(
        body,
        mesh=mesh,
        in_specs=(P("ctx", None), P(None, "head"), P("head", None), P(None, "ctx", None), P(None, "ctx", None),
                  P(None, "ctx", None), P(None, "ctx", None), P(), P()),
        out_specs=P("ctx", "head"),
        check_vma=False,
    )
```

```python
import functools

import jax
import jax.numpy as jnp
from jax import lax
from jax.experimental import pallas as pl
from jax.experimental.pallas import tpu as pltpu
from jax.sharding import PartitionSpec as P

JSPAN = 32
ROPE_BASE = 500000.0
LOG2E = 1.4426950408889634
HIDE = 1e30
CHUNK = 512
SHARES = 2
MIB = 1 << 20


def rope_tables(rows, width, first, scale):
    half = width // 2
    freq = ROPE_BASE ** (-(jnp.arange(half, dtype=jnp.float32) * 2.0) / width)
    place = (first + jnp.arange(rows)).astype(jnp.float32)
    angle = place[:, None] * freq[None, :]
    cosine = jnp.cos(angle) * scale
    sine = jnp.sin(angle) * scale
    return jnp.concatenate([cosine, cosine], axis=1), jnp.concatenate([-sine, sine], axis=1)


def attend_kernel(per_kv, blocks_each, share, shares, n_ctx, at_ref, lengths_ref, seen_ref, q_ref, ok_ref, ov_ref, bk_ref, bv_ref,
                  o_ref, stat_ref, ok_turned, bk_turned, ov_wide, bv_wide, order):
    width = ok_ref.shape[2]
    me = at_ref[1]
    length = lengths_ref[me]
    blocks = q_ref.shape[0] // JSPAN
    each = blocks // n_ctx
    branch_most = bk_ref.shape[1]
    chunk = min(CHUNK, branch_most)
    ok_turned[...] = ok_ref[0].T
    for part in range(branch_most // chunk):
        bk_turned[part] = bk_ref[0, part * chunk:(part + 1) * chunk].T
    ov_wide[:, :width] = ov_ref[0]
    ov_wide[:, width:] = jnp.ones((ov_ref.shape[1], width), jnp.bfloat16)
    bv_wide[:, :width] = bv_ref[0]
    bv_wide[:, width:] = jnp.ones((branch_most, width), jnp.bfloat16)

    def place(block, ends):
        front, back = ends
        hit = seen_ref[(block // each) * (each * shares) + share * each + block % each, me] == 1
        order[jnp.where(hit, front, back)] = block
        step = hit.astype(jnp.int32)
        return front + step, back - 1 + step

    seen_count, _ = lax.fori_loop(0, blocks, place, (jnp.int32(0), jnp.int32(blocks - 1)))

    tile = blocks_each * JSPAN
    chunks = branch_most // chunk

    def turn(step, _):
        base = step * blocks_each
        starts = [pl.multiple_of(order[base + j] * JSPAN, JSPAN) for j in range(blocks_each)]

        def go_heads(live, heads):
            query = jnp.concatenate(
                [q_ref[pl.ds(at, JSPAN), h * width:(h + 1) * width] for h in heads for at in starts], axis=0)
            s = jnp.dot(query, ok_turned[...], preferred_element_type=jnp.float32)
            best = jnp.max(s, axis=1, keepdims=True)
            lower = best
            found = []
            if live > 0:
                row = lax.broadcasted_iota(jnp.int32, (len(heads) * tile, 1), 0)
                shown = (row & (tile - 1)) < (seen_count - base) * JSPAN
                for part in range(live):
                    more = jnp.dot(query, bk_turned[part], preferred_element_type=jnp.float32)
                    if part == live - 1:
                        place_in = part * chunk + lax.broadcasted_iota(jnp.int32, (1, chunk), 1)
                        more = more + jnp.where(place_in < length, 0.0, -HIDE)
                    found.append(more)
                grown = best
                for more in found:
                    grown = jnp.maximum(grown, jnp.max(more, axis=1, keepdims=True))
                best = jnp.where(shown, grown, best)
                lower = jnp.where(shown, grown, HIDE)
            acc = jnp.dot(jnp.exp2(s - best).astype(jnp.bfloat16), ov_wide[...], preferred_element_type=jnp.float32)
            for part, more in enumerate(found):
                weights = jnp.exp2(more - lower).astype(jnp.bfloat16)
                acc += jnp.dot(weights, bv_wide[part * chunk:(part + 1) * chunk], preferred_element_type=jnp.float32)
            total = acc[:, width:]
            part_out = (acc[:, :width] / total).astype(o_ref.dtype)
            logs = best + jnp.log2(total[:, :1])
            for h in heads:
                for j in range(blocks_each):
                    here = ((h - heads[0]) * blocks_each + j) * JSPAN
                    rows = pl.ds(starts[j], JSPAN)
                    o_ref[rows, h * width:(h + 1) * width] = part_out[here:here + JSPAN]
                    stat_ref[0, rows, h:h + 1] = logs[here:here + JSPAN]

        def go(live):
            half = max(1, per_kv // 2)
            for low in range(0, per_kv, half):
                go_heads(live, range(low, min(low + half, per_kv)))

        needed = jnp.where(base < seen_count, (length + chunk - 1) // chunk, 0)
        for live in range(chunks + 1):
            pl.when(needed == live)(functools.partial(go, live))
        return 0

    lax.fori_loop(0, blocks // blocks_each, turn, 0)


def attend(query, share, shares, n_ctx, kv_local, kv, me, lengths, seen, outline_keys, outline_values, branch_keys, branch_values):
    rows, columns = query.shape
    width = outline_keys.shape[2]
    per_kv = columns // (width * kv_local)
    outline_here, branch_most = outline_keys.shape[1], branch_keys.shape[1]
    mine = lambda i, at, lens, vis: (0, i)
    one = lambda i, at, lens, vis: (at[0] + i, 0, 0)
    keys_all = outline_here + branch_most // 2
    return pl.pallas_call(
        functools.partial(attend_kernel, per_kv, 4, share, shares, n_ctx),
        out_shape=(jax.ShapeDtypeStruct((rows, columns), jnp.bfloat16), jax.ShapeDtypeStruct((kv_local, rows, per_kv), jnp.float32)),
        grid_spec=pltpu.PrefetchScalarGridSpec(
            num_scalar_prefetch=3,
            grid=(kv_local,),
            in_specs=[
                pl.BlockSpec((rows, per_kv * width), mine),
                pl.BlockSpec((1, outline_here, width), one),
                pl.BlockSpec((1, outline_here, width), one),
                pl.BlockSpec((1, branch_most, width), one),
                pl.BlockSpec((1, branch_most, width), one),
            ],
            out_specs=(pl.BlockSpec((rows, per_kv * width), mine), pl.BlockSpec((1, rows, per_kv), lambda i, at, lens, vis: (i, 0, 0))),
            scratch_shapes=[
                pltpu.VMEM((width, outline_here), jnp.bfloat16),
                pltpu.VMEM((branch_most // min(CHUNK, branch_most), width, min(CHUNK, branch_most)), jnp.bfloat16),
                pltpu.VMEM((outline_here, 2 * width), jnp.bfloat16),
                pltpu.VMEM((branch_most, 2 * width), jnp.bfloat16),
                pltpu.SMEM((rows // JSPAN,), jnp.int32),
            ],
        ),
        compiler_params=pltpu.CompilerParams(vmem_limit_bytes=60 * MIB),
        cost_estimate=pl.CostEstimate(
            flops=rows * columns * keys_all * 8, bytes_accessed=4 * rows * columns, transcendentals=rows * per_kv * kv_local * keys_all),
        name="attend",
    )(jnp.stack([kv, me]).astype(jnp.int32), lengths, seen, query, outline_keys, outline_values, branch_keys, branch_values)


def return_kernel(n_ctx, kv_local, heads, *refs):
    parts = refs[:kv_local]
    logs_ref, mixed_ref, near, near_logs, joined, joined_logs, far, far_logs = refs[kv_local:kv_local + 8]
    near_sems, far_sems = refs[kv_local + 8:]
    rows, columns = near.shape[2:]
    width = kv_local * columns // heads
    per_kv = columns // width
    chips = n_ctx // 2
    me = lax.axis_index("ctx")
    chip, core = me // 2, me % 2
    sibling = chip * 2 + 1 - core

    def peer(j):
        return ((chip + j) % chips) * 2

    def copy(src, dst, sems, which, device):
        return pltpu.make_async_remote_copy(
            src_ref=src, dst_ref=dst, send_sem=sems.at[0, which], recv_sem=sems.at[1, which],
            device_id={"ctx": device}, device_id_type=pl.DeviceIdType.MESH)

    barrier = pltpu.get_barrier_semaphore()
    pl.semaphore_signal(barrier, inc=1, device_id={"ctx": sibling}, device_id_type=pl.DeviceIdType.MESH)
    for j in range(1, chips):
        pl.semaphore_signal(barrier, inc=1, device_id={"ctx": peer(j) + core}, device_id_type=pl.DeviceIdType.MESH)
    pl.semaphore_wait(barrier, chips)

    def spread(shares):
        filled = jnp.concatenate([shares, jnp.zeros((128 - shares.shape[0], rows), jnp.float32)], axis=0)
        return filled.T

    sequence = [(j + 1) % chips for j in range(chips)]
    sequence = sequence[::-1][1:] + [0] if chips > 1 else sequence
    near_copies = {}
    for j in sequence:
        block = peer(j) + 1 - core
        mine = pl.ds(pl.multiple_of(block * rows, rows), rows)
        group = [copy(logs_ref.at[block], near_logs.at[j], near_sems, j * (kv_local + 1) + kv_local, sibling)]
        for kv in range(kv_local):
            group.append(copy(parts[kv].at[mine], near.at[j, kv], near_sems, j * (kv_local + 1) + kv, sibling))
        for c in group:
            c.start()
        near_copies[j] = group
    far_copies = {}
    for j in sequence:
        for c in near_copies[j]:
            c.wait_recv()
        block = peer(j) + core
        own, other = logs_ref[block], near_logs[j]
        top = jnp.maximum(own, other)
        own_share, other_share = jnp.exp2(own - top), jnp.exp2(other - top)
        total = own_share + other_share
        joined_logs[j] = top + jnp.log2(total)
        own_wide, other_wide = spread(own_share / total), spread(other_share / total)
        mine = pl.ds(pl.multiple_of(block * rows, rows), rows)
        for kv in range(kv_local):
            for h in range(per_kv):
                at, head = slice(h * width, (h + 1) * width), kv * per_kv + h
                value = (parts[kv][mine, at].astype(jnp.float32) * own_wide[:, head:head + 1]
                         + near[j, kv, :, at].astype(jnp.float32) * other_wide[:, head:head + 1])
                joined[j, kv, :, at] = value.astype(jnp.bfloat16)
        if j > 0:
            group = [copy(joined_logs.at[j], far_logs.at[j - 1], far_sems, 2 * (j - 1) + 1, peer(j) + core),
                     copy(joined.at[j], far.at[j - 1], far_sems, 2 * (j - 1), peer(j) + core)]
            for c in group:
                c.start()
            far_copies[j] = group
    for j in range(1, chips):
        for c in far_copies[j]:
            c.wait_recv()
    every = [joined_logs[0]] + [far_logs[j] for j in range(chips - 1)]
    top = functools.reduce(jnp.maximum, every)
    shares = [jnp.exp2(x - top) for x in every]
    total = functools.reduce(jnp.add, shares)
    wide = [spread(x / total) for x in shares]
    for kv in range(kv_local):
        for h in range(per_kv):
            at, head = slice(h * width, (h + 1) * width), kv * per_kv + h
            value = joined[0, kv, :, at].astype(jnp.float32) * wide[0][:, head:head + 1]
            for j in range(chips - 1):
                value += far[j, kv, :, at].astype(jnp.float32) * wide[j + 1][:, head:head + 1]
            mixed_ref[:, head * width:(head + 1) * width] = value.astype(jnp.bfloat16)
    for j in sequence:
        for c in near_copies[j] + far_copies.get(j, []):
            c.wait_send()


def give_back(parts, logs, n_ctx, heads, number):
    kv_local = len(parts)
    rows, columns = parts[0].shape[0] // n_ctx, parts[0].shape[1]
    chips = n_ctx // 2
    fars = max(chips - 1, 1)
    tall = logs.shape[1]
    vmem = pl.BlockSpec(memory_space=pltpu.VMEM)
    return pl.pallas_call(
        functools.partial(return_kernel, n_ctx, kv_local, heads),
        out_shape=jax.ShapeDtypeStruct((rows, kv_local * columns), jnp.bfloat16),
        in_specs=[vmem] * (kv_local + 1),
        out_specs=vmem,
        scratch_shapes=[
            pltpu.VMEM((chips, kv_local, rows, columns), jnp.bfloat16),
            pltpu.VMEM((chips, tall, rows), jnp.float32),
            pltpu.VMEM((chips, kv_local, rows, columns), jnp.bfloat16),
            pltpu.VMEM((chips, tall, rows), jnp.float32),
            pltpu.VMEM((fars, kv_local, rows, columns), jnp.bfloat16),
            pltpu.VMEM((fars, tall, rows), jnp.float32),
            pltpu.SemaphoreType.DMA((2, chips * (kv_local + 1))),
            pltpu.SemaphoreType.DMA((2, 2 * fars)),
        ],
        compiler_params=pltpu.CompilerParams(collective_id=number, has_side_effects=True, vmem_limit_bytes=40 * MIB),
        name="give_back",
    )(*parts, logs)


def body(join_states, query_weight, out_weight, outline_keys, outline_values, branch_keys, branch_values, branch_lengths, visibility):
    width = outline_keys.shape[2]
    head_count = query_weight.shape[1] // width
    group = head_count * lax.axis_size("head") // outline_keys.shape[0]
    kv_local = max(1, head_count // group)
    per_kv = head_count // kv_local
    kv_start = lax.axis_index("head") * head_count // group
    rows = join_states.shape[0]
    n_ctx = lax.axis_size("ctx")
    me = lax.axis_index("ctx")
    first = outline_keys.shape[1] * n_ctx + branch_keys.shape[1] + me * rows
    cosine, sine = rope_tables(rows, width, first, width ** (-0.5) * LOG2E)
    shares = SHARES
    some = rows // shares
    gathered = []
    for share in range(shares):
        mine = slice(share * some, (share + 1) * some)
        queries = jnp.dot(join_states[mine], query_weight, preferred_element_type=jnp.float32)
        queries = queries.reshape(some, head_count, width)
        turned = jnp.concatenate([queries[..., width // 2:], queries[..., :width // 2]], axis=-1)
        rotated = (queries * cosine[mine, None, :] + turned * sine[mine, None, :]).astype(jnp.bfloat16)
        gathered.append(lax.all_gather(rotated.reshape(some, head_count * width), "ctx", axis=0, tiled=True))
    outs = []
    partial_out = None
    for share in range(shares):
        query = gathered[share]
        if share > 0:
            query, partial_out = lax.optimization_barrier((query, partial_out))
            outs.append(lax.psum_scatter(partial_out, "head", scatter_dimension=1, tiled=True))
        part, logs = attend(query, share, shares, n_ctx, kv_local, kv_start, me, branch_lengths, visibility,
                            outline_keys, outline_values, branch_keys, branch_values)
        if share > 0:
            part, outs[-1] = lax.optimization_barrier((part, outs[-1]))
        logs = logs.reshape(kv_local, n_ctx, some, per_kv).transpose(1, 0, 3, 2).reshape(n_ctx, head_count, some)
        logs = jnp.pad(logs, ((0, 0), (0, -head_count % 8), (0, 0)))
        mixed = give_back([part], logs, n_ctx, head_count, share + 1)
        partial_out = jnp.dot(mixed, out_weight, preferred_element_type=jnp.float32).astype(jnp.bfloat16)
    outs.append(lax.psum_scatter(partial_out, "head", scatter_dimension=1, tiled=True))
    return jnp.concatenate(outs, axis=0)


def solution(mesh):
    return jax.shard_map(
        body,
        mesh=mesh,
        in_specs=(P("ctx", None), P(None, "head"), P("head", None), P(None, "ctx", None), P(None, "ctx", None),
                  P(None, "ctx", None), P(None, "ctx", None), P(), P()),
        out_specs=P("ctx", "head"),
        check_vma=False,
    )
```
